32 devices in a mesh: lat: 8 (over y, x, core), lon: 4 (over z).
Axes of the slice: x: 2, y: 2, z: 4, core: 2. Of those that a mesh axis runs over, the one named last changes fastest.
Arguments:
- state_field: float32 [96, 96, 256], P('lat', 'lon'), may hold values from -6 to 6
- cotangent: bfloat16 [96, 96, 256], P('lat', 'lon'), may hold values from -6 to 6
- depthwise: float32 [49, 256], replicated, may hold values from -0.875 to 0.875
- norm_gain: float32 [256], replicated, may hold values from 0.4 to 1.6
- w_in: bfloat16 [256, 1024], replicated, may hold values from -0.375 to 0.375
- w_out: bfloat16 [1024, 256], replicated, may hold values from -0.1875 to 0.1875
Outputs:
- block_out: bfloat16 [96, 96, 256], P('lat', 'lon')
- grad_input: bfloat16 [96, 96, 256], P('lat', 'lon')
- weight_grads: float32 [1024, 512], P(('lat', 'lon'))
- grad_depthwise: float32 [49, 256], replicated
- grad_gain: float32 [256], replicated
The draws below stay inside these ranges and needn't reach their ends.
All inputs are finite; a program needn't handle non-finite values.
Results may differ from the reference program's by a relative error of at most 0.0052.
Values sent between devices are 32-bit elements; how exact they have to be, the bound alone decides.
A program may use at most 64 MiB of HBM per device.

```python
import math
import jax
import jax.numpy as jnp
from jax import lax

C = 256
FF = 1024
NLAT = 96
NLON = 96


def level_of(stream_key, dims, split, least, high):
    gain, own = 1.0, jax.random.fold_in(stream_key, 6)
    for position, shards_of in split:
        draws = jnp.exp(jax.random.uniform(jax.random.fold_in(own, position), (shards_of,), jnp.float32, least / len(split), high / len(split)))
        gain = gain * jnp.repeat(draws, dims[position] // shards_of).reshape([-1 if axis == position else 1 for axis in range(len(dims))])
    return gain


def bell_draw(own_key, dims, spread, reach, pieces=(), kind=jnp.bfloat16):
    gain = level_of(own_key, dims, pieces, -0.22, 0.18) if pieces else 1.0
    entries = jax.random.normal(own_key, dims, jnp.float32) * spread * gain
    return jnp.minimum(jnp.maximum(entries, -reach), reach).astype(kind)


def setup_inputs(seed: int = 0) -> dict:
    seeds = jax.random.split(jax.random.key(seed), 7)
    return {
        "state_field": bell_draw(seeds[0], (NLAT, NLON, C), 1.0, 6.0, ((0, 8), (1, 4)), jnp.float32),
        "cotangent": bell_draw(seeds[1], (NLAT, NLON, C), 1.0, 6.0, ((0, 8), (1, 4))),
        "depthwise": bell_draw(seeds[2], (49, C), 49 ** -0.5, 0.875, (), jnp.float32),
        "norm_gain": jnp.clip(1.0 + 0.12 * jax.random.normal(seeds[3], (C,), jnp.float32), 0.4, 1.6),
        "w_in": bell_draw(seeds[4], (C, FF), C ** -0.5, 0.375),
        "w_out": bell_draw(seeds[5], (FF, C), FF ** -0.5, 0.1875),
    }


def gelu_value(values):
    return 0.5 * values * (1.0 + lax.erf(values * 0.7071067811865476))

def gelu_slope(values):
    return 0.5 * (1.0 + lax.erf(values * 0.7071067811865476)) + values * jnp.exp(-0.5 * values * values) * 0.3989422804014327

def layer_norm(convolved, norm_gain):
    average = lax.optimization_barrier(jnp.mean(convolved, axis=-1, keepdims=True))
    centred_raw = convolved - average
    variance = lax.optimization_barrier(jnp.mean(centred_raw * centred_raw, axis=-1, keepdims=True))
    inv_std = 1.0 / jnp.sqrt(variance + 1e-06)
    centred = centred_raw * inv_std
    normed = (centred * norm_gain).astype(jnp.bfloat16)
    return (normed, centred, inv_std)

def extend(state_field, half_turn):
    top_rows = jnp.roll(jnp.flip(state_field[:3], 0), -half_turn, axis=1)
    bottom_rows = jnp.roll(jnp.flip(state_field[-3:], 0), -half_turn, axis=1)
    tall = jnp.concatenate([top_rows, state_field, bottom_rows], 0)
    return jnp.concatenate([tall[:, -3:], tall, tall[:, :3]], 1)

def apply_taps(extended, depthwise, lat_rows, lon_cols):
    running = jnp.zeros((lat_rows, lon_cols, extended.shape[2]), jnp.float32)
    for row_off in range(7):
        for col_off in range(7):
            running = running + depthwise[7 * row_off + col_off] * extended[row_off:row_off + lat_rows, col_off:col_off + lon_cols]
    return running

def adjoint_taps(grad_conv, depthwise, lat_rows, lon_cols):
    padded = jnp.pad(grad_conv, ((6, 6), (6, 6), (0, 0)))
    running = jnp.zeros((lat_rows + 6, lon_cols + 6, grad_conv.shape[2]), jnp.float32)
    for row_off in range(7):
        for col_off in range(7):
            running = running + depthwise[7 * row_off + col_off] * padded[6 - row_off:12 - row_off + lat_rows, 6 - col_off:12 - col_off + lon_cols]
    return running

def fold(tap_grid, half_turn):
    interior = tap_grid[:, 3:-3]
    interior = interior.at[:, :3].add(tap_grid[:, -3:]).at[:, -3:].add(tap_grid[:, :3])
    inner = interior[3:-3]
    inner = inner.at[:3].add(jnp.flip(jnp.roll(interior[:3], half_turn, axis=1), 0))
    inner = inner.at[-3:].add(jnp.flip(jnp.roll(interior[-3:], half_turn, axis=1), 0))
    return inner

def reference(state_field, cotangent, depthwise, norm_gain, w_in, w_out):
    lat_rows, lon_cols, channels = state_field.shape
    unit_count = w_in.shape[1]
    half_turn = lon_cols // 2
    grad_scale = 1.0 / math.sqrt(lat_rows * lon_cols)
    extended = extend(state_field, half_turn)
    convolved = apply_taps(extended, depthwise, lat_rows, lon_cols)

    def row_step(running, inputs):
        unit_sum, gain_sum = running
        conv_row, field_row, cot_row = inputs
        normed, centred, inv_std = layer_norm(conv_row, norm_gain)
        pre_act = jnp.dot(normed, w_in, preferred_element_type=jnp.float32)
        hidden = gelu_value(pre_act).astype(jnp.bfloat16)
        branch = jnp.dot(hidden, w_out, preferred_element_type=jnp.float32)
        out_row = (field_row + branch).astype(jnp.bfloat16)
        grad_hidden = jnp.dot(cot_row, w_out.T, preferred_element_type=jnp.float32)
        grad_pre = (grad_hidden * gelu_slope(pre_act)).astype(jnp.bfloat16)
        grad_normed = jnp.dot(grad_pre, w_in.T, preferred_element_type=jnp.float32)
        scaled_grad = grad_normed * norm_gain
        grad_conv = inv_std * (scaled_grad - lax.optimization_barrier(jnp.mean(scaled_grad, axis=-1, keepdims=True)) - centred * lax.optimization_barrier(jnp.mean(scaled_grad * centred, axis=-1, keepdims=True)))
        weight_terms = jnp.concatenate([jnp.dot(grad_pre.T, normed, preferred_element_type=jnp.float32), jnp.dot(hidden.T, cot_row, preferred_element_type=jnp.float32)], 1)
        gain_terms = lax.optimization_barrier(jnp.sum(grad_normed * centred, axis=0))
        return ((unit_sum + weight_terms, gain_sum + gain_terms), (out_row, grad_conv))
    initial = (jnp.zeros((unit_count, 2 * channels), jnp.float32), jnp.zeros((channels,), jnp.float32))
    (unit_sum, gain_sum), (block_out, grad_conv) = lax.scan(row_step, initial, (convolved, state_field, cotangent))
    tap_grid = adjoint_taps(grad_conv, depthwise, lat_rows, lon_cols)
    grad_input = (cotangent.astype(jnp.float32) + fold(tap_grid, half_turn)).astype(jnp.bfloat16)
    tap_list = []
    for row_off in range(7):
        for col_off in range(7):
            tap_list.append(lax.optimization_barrier(jnp.sum(extended[row_off:row_off + lat_rows, col_off:col_off + lon_cols] * grad_conv, axis=(0, 1))))
    grad_depthwise = jnp.stack(tap_list, 0) * grad_scale
    return (block_out, grad_input, unit_sum * grad_scale, grad_depthwise, gain_sum * grad_scale)
```

```python
import functools
import math

import jax
import jax.numpy as jnp
from jax import lax
from jax.experimental import pallas as pl
from jax.experimental.pallas import tpu as pltpu
from jax.sharding import PartitionSpec as P

MESH = pl.DeviceIdType.MESH
F32 = jnp.float32
BF16 = jnp.bfloat16
SIDE = 8
CHUNK = 256
TAP_HALF = 32


def dot(left, right, dims):
    return lax.dot_general(left, right, (dims, ((), ())), preferred_element_type=F32)


def bits_of(size):
    return size.bit_length() - 1


def kernel(
    n_lat, n_lon,
    state, cot, taps, gain, w_in, w_out,
    out, gin, wgrad, gtaps, ggain,
    ext, rims, shifts, gext, grims, gshifts, conv, centred_s, istd_s, normed_s, cot_s,
    branch_s, gnorm_s, turned, local_w, core_w, tap_mine, tap_far, tap_sum, tap_done,
    r_own, r_got, l_own, l_got, t_got,
    halo_send, halo_recv, core_send, core_recv, ring_send, ring_recv, tap_send, tap_recv,
):
    height, width, channels = state.shape
    cells = height * width
    units = w_in.shape[1]
    rows = units // (n_lat * n_lon)
    block = n_lon * rows
    half_blocks = n_lat // 2
    lat, lon = lax.axis_index("lat"), lax.axis_index("lon")
    first, last = lat == 0, lat == n_lat - 1
    core = lax.rem(lat, 2)

    def wrap(value):
        return lax.rem(value + 2 * n_lon, n_lon)

    up_lat = jnp.where(first, 0, lat - 1)
    down_lat = jnp.where(last, n_lat - 1, lat + 1)
    up_off = jnp.where(first, n_lon // 2, 0)
    down_off = jnp.where(last, n_lon // 2, 0)
    up_side = jnp.where(first, 0, 1)
    down_side = jnp.where(last, 1, 0)

    def flip_bit(index, bit):
        size = 1 << bit
        mine = lax.rem(lax.div(index, size), 2)
        return index + size - 2 * size * mine, mine

    def lat_peer(bit):
        peer, mine = flip_bit(lat, bit)
        return (peer, lon), mine

    def lon_peer(bit):
        peer, mine = flip_bit(lon, bit)
        return (lat, peer), mine

    core_peer, _ = lat_peer(0)

    peers = []
    for side in (-1, 0, 1):
        peers.append((up_lat, wrap(lon + up_off + side)))
        peers.append((down_lat, wrap(lon + down_off + side)))
    peers.append((lat, wrap(lon - 1)))
    peers.append((lat, wrap(lon + 1)))
    for bit in range(bits_of(n_lat)):
        peers.append(lat_peer(bit)[0])
    for bit in range(bits_of(n_lon)):
        peers.append(lon_peer(bit)[0])
    barrier = pltpu.get_barrier_semaphore()
    for peer in peers:
        pl.semaphore_signal(barrier, inc=1, device_id=peer, device_id_type=MESH)
    pl.semaphore_wait(barrier, len(peers))

    def remote(source, target, send, recv, peer):
        return pltpu.make_async_remote_copy(
            src_ref=source, dst_ref=target, send_sem=send, recv_sem=recv,
            device_id=peer, device_id_type=MESH,
        )

    spans = ((-1, 0, SIDE), (0, 0, width), (1, width - SIDE, SIDE))
    places = ((-1, SIDE + width), (0, SIDE), (1, 0))

    def halo_copies(stage, source, whole, rim):
        copies = []
        for number, ((side, start, count), (_, place)) in enumerate(zip(spans, places)):
            for end, (peer_lat, off, slot) in enumerate(
                ((up_lat, up_off, up_side), (down_lat, down_off, down_side))
            ):
                begin = 0 if end == 0 else height - 3
                copies.append(
                    remote(
                        source.at[pl.ds(begin, 3), pl.ds(start, count)],
                        rim.at[slot, :, pl.ds(place, count)],
                        halo_send.at[stage, 2 * number + end],
                        halo_recv.at[stage, 2 * number + slot],
                        (peer_lat, wrap(lon + off + side)),
                    )
                )
        copies.append(
            remote(
                source.at[:, pl.ds(0, SIDE)], whole.at[pl.ds(3, height), pl.ds(SIDE + width, SIDE)],
                halo_send.at[stage, 6], halo_recv.at[stage, 6], (lat, wrap(lon - 1)),
            )
        )
        copies.append(
            remote(
                source.at[:, pl.ds(width - SIDE, SIDE)], whole.at[pl.ds(3, height), pl.ds(0, SIDE)],
                halo_send.at[stage, 7], halo_recv.at[stage, 7], (lat, wrap(lon + 1)),
            )
        )
        return copies

    def finish_halo(stage, source, whole, rim, shifted):
        copies = halo_copies(stage, source, whole, rim)
        for copy in copies:
            copy.wait_send()
        for copy in copies[6:]:
            copy.wait_recv()
        for number, ((_, start, count), (_, place)) in enumerate(zip(spans, places)):
            for slot in range(2):
                remote(
                    source.at[pl.ds(0, 3), pl.ds(start, count)],
                    rim.at[slot, :, pl.ds(place, count)],
                    halo_send.at[stage, 2 * number + slot],
                    halo_recv.at[stage, 2 * number + slot],
                    (lat, wrap(lon + 1)),
                ).wait_recv()
        for row in range(3):
            whole[row] = jnp.where(first, rim[0, 2 - row], rim[0, row])
            whole[height + 3 + row] = jnp.where(last, rim[1, 2 - row], rim[1, row])

        def shift_row(row, carry):
            for col in range(7):
                shifted[col, row] = whole[row, pl.ds(SIDE - 3 + col, width), :]
            return carry

        lax.fori_loop(0, height + 6, shift_row, 0)

    for copy in halo_copies(0, state, ext, rims):
        copy.start()

    ext[pl.ds(3, height), pl.ds(SIDE, width), :] = state[...]
    cot_s[...] = cot[...].astype(F32).reshape(cells, channels).astype(BF16)
    branch_s[...] = jnp.zeros_like(branch_s)
    gnorm_s[...] = jnp.zeros_like(gnorm_s)
    for row in range(7):
        for col in range(7):
            plain = taps[pl.ds(48 - 7 * row - col, 1), :]
            mirrored = taps[pl.ds(7 * row + 6 - col, 1), :]
            spot = pl.ds(7 * row + col, 1)
            turned[0, spot, :] = jnp.where(first, mirrored, plain)
            turned[1, spot, :] = plain
            turned[2, spot, :] = jnp.where(last, mirrored, plain)

    finish_halo(0, state, ext, rims, shifts)

    def conv_row(index, carry):
        total = jnp.zeros((width, channels), F32)
        for row in range(7):
            for col in range(7):
                total = total + shifts[col, index + row] * taps[pl.ds(7 * row + col, 1), :]
        conv[index] = total
        return carry

    lax.fori_loop(0, height, conv_row, 0)

    flat = conv[...].reshape(cells, channels)
    raw = flat - jnp.mean(flat, axis=-1, keepdims=True)
    inv_std = 1.0 / jnp.sqrt(jnp.mean(raw * raw, axis=-1, keepdims=True) + 1e-06)
    centred = raw * inv_std
    istd_s[...] = inv_std
    centred_s[...] = centred
    normed_s[...] = (centred * gain[...]).astype(BF16)

    per_chunk = CHUNK // (2 * block)

    def core_copy(chunk):
        span = pl.ds(chunk * per_chunk, per_chunk)
        return remote(
            local_w.at[span, 1 - core], core_w.at[span],
            core_send.at[chunk], core_recv.at[chunk], core_peer,
        )

    def unit_chunk(chunk, carry):
        span = pl.ds(pl.multiple_of(chunk * CHUNK, CHUNK), CHUNK)
        into = w_in[:, span]
        outof = w_out[span, :]
        pre = dot(normed_s[...], into, ((1,), (0,)))
        share = 0.5 * (1.0 + lax.erf(pre * 0.7071067811865476))
        hidden = (pre * share).astype(BF16)
        slope = share + pre * jnp.exp(-0.5 * pre * pre) * 0.3989422804014327
        grad_pre = (dot(cot_s[...], outof, ((1,), (1,))) * slope).astype(BF16)
        left = dot(grad_pre, normed_s[...], ((0,), (0,)))
        right = dot(hidden, cot_s[...], ((0,), (0,)))
        blocks = pl.ds(chunk * per_chunk, per_chunk)
        local_w[blocks, :, :, pl.ds(0, channels)] = left.reshape(per_chunk, 2, block, channels)
        local_w[blocks, :, :, pl.ds(channels, channels)] = right.reshape(
            per_chunk, 2, block, channels
        )
        core_copy(chunk).start()
        branch_s[...] += dot(hidden, outof, ((1,), (0,)))
        gnorm_s[...] += dot(grad_pre, into, ((1,), (1,)))
        return carry

    lax.fori_loop(0, units // CHUNK, unit_chunk, 0)

    gnorm = gnorm_s[...]
    centred = centred_s[...]
    scaled = gnorm * gain[...]
    grad_conv = istd_s[...] * (
        scaled
        - jnp.mean(scaled, axis=-1, keepdims=True)
        - centred * jnp.mean(scaled * centred, axis=-1, keepdims=True)
    )
    conv[...] = grad_conv.reshape(height, width, channels)
    for copy in halo_copies(1, conv, gext, grims):
        copy.start()
    gext[pl.ds(3, height), pl.ds(SIDE, width), :] = conv[...]
    tap_mine[1, pl.ds(TAP_HALF // 2, TAP_HALF // 2), :] = jnp.zeros((TAP_HALF // 2, channels), F32)
    tap_mine[1, pl.ds(49 - TAP_HALF, 1), :] = jnp.sum(gnorm * centred, axis=0, keepdims=True)

    lat_bits = list(range(1, bits_of(n_lat)))
    lon_bits = list(range(bits_of(n_lon)))
    r_steps = [("lat", bit) for bit in lat_bits] + [("lon", bit) for bit in lon_bits]
    l_steps = [("lat", bit) for bit in lat_bits[::-1]] + [("lon", bit) for bit in lon_bits]

    def peer_of(step):
        return lat_peer(step[1]) if step[0] == "lat" else lon_peer(step[1])

    def ring_copy(stream, own, got, steps, number):
        peer, mine = peer_of(steps[number])
        low = stream == 0 or steps[number][0] == "lon"
        source = own[number].at[:, 1 - mine] if low else own[number].at[1 - mine]
        return remote(
            source, got[number], ring_send.at[stream, number], ring_recv.at[stream, number], peer
        )

    def store_own(own, number, index, value, steps, stream):
        step = steps[number]
        low = stream == 0 or step[0] == "lon"
        if low:
            own[number][index // 2, index % 2] = value
        else:
            count = own[number].shape[1]
            own[number][index // count, index % count] = value

    def place(own, number, steps, stream, pieces):
        if steps[number][0] == "lon" and (number == 0 or steps[number - 1][0] == "lat"):
            (piece,) = pieces
            pieces = [piece[rows * part : rows * (part + 1)] for part in range(n_lon)]
        for index, value in enumerate(pieces):
            store_own(own, number, index, value, steps, stream)

    def ring_sum(stream, own, got, steps, number):
        _, mine = peer_of(steps[number])
        low = stream == 0 or steps[number][0] == "lon"
        pieces = []
        for index in range(got[number].shape[0]):
            kept = own[number][index, mine] if low else own[number][mine, index]
            pieces.append(kept + got[number][index])
        return pieces

    for chunk in range(units // CHUNK):
        core_copy(chunk).wait()
    for stream, own, got, steps, begin in (
        (0, r_own, r_got, r_steps, channels), (1, l_own, l_got, l_steps, 0)
    ):
        pieces = [
            local_w[index, core, :, pl.ds(begin, channels)]
            + core_w[index, :, pl.ds(begin, channels)]
            for index in range(half_blocks)
        ]
        place(own, 0, steps, stream, pieces)
        ring_copy(stream, own, got, steps, 0).start()

    out[...] = (
        state[...] + branch_s[...].reshape(height, width, channels)
    ).astype(BF16)

    def tap_row(index, carry):
        row, col = lax.div(index, 7), lax.rem(index, 7)
        total = jnp.zeros((width, channels), F32)
        for line in range(height):
            total = total + shifts[col, row + line] * conv[line]
        tap_mine[lax.div(index, TAP_HALF), pl.ds(lax.rem(index, TAP_HALF), 1), :] = jnp.sum(
            total, axis=0, keepdims=True
        )
        return carry

    lax.fori_loop(0, 49, tap_row, 0)
    tap_first = remote(
        tap_mine.at[1 - core], tap_far, tap_send.at[0], tap_recv.at[0], core_peer
    )
    tap_first.start()

    finish_halo(1, conv, gext, grims, gshifts)

    def adjoint_row(index, carry):
        total = jnp.zeros((width, channels), F32)
        for row in range(7):
            line = index + row
            kind = jnp.where(line < 3, 0, jnp.where(line >= height + 3, 2, 1))
            for col in range(7):
                total = total + gshifts[col, line] * turned[kind, pl.ds(7 * row + col, 1), :]
        ext[index, pl.ds(0, width), :] = total
        return carry

    lax.fori_loop(0, height, adjoint_row, 0)
    gin[...] = (cot[...].astype(F32) + ext[pl.ds(0, height), pl.ds(0, width), :]).astype(BF16)

    tap_first.wait()
    tap_sum[0] = tap_mine[core] + tap_far[...]

    def tap_copy(number):
        peer, _ = peer_of(r_steps[number])
        return remote(
            tap_sum.at[number], t_got.at[number],
            tap_send.at[1 + number], tap_recv.at[1 + number], peer,
        )

    scale = 1.0 / math.sqrt(cells * n_lat * n_lon)
    tap_copy(0).start()
    count = len(r_steps)
    for number in range(count):
        for stream, own, got, steps, begin in (
            (0, r_own, r_got, r_steps, channels), (1, l_own, l_got, l_steps, 0)
        ):
            ring_copy(stream, own, got, steps, number).wait()
            pieces = ring_sum(stream, own, got, steps, number)
            if number < count - 1:
                place(own, number + 1, steps, stream, pieces)
                ring_copy(stream, own, got, steps, number + 1).start()
            else:
                wgrad[:, pl.ds(begin, channels)] = pieces[0] * scale
        tap_copy(number).wait()
        total = tap_sum[number] + t_got[number]
        if number < count - 1:
            tap_sum[number + 1] = total
            tap_copy(number + 1).start()
        else:
            tap_done[core] = total * scale
    tap_last = remote(
        tap_done.at[core], tap_done.at[core],
        tap_send.at[1 + count], tap_recv.at[1 + count], core_peer,
    )
    tap_last.start()
    tap_last.wait()
    gtaps[pl.ds(0, TAP_HALF), :] = tap_done[0]
    gtaps[pl.ds(TAP_HALF, 49 - TAP_HALF), :] = tap_done[1, pl.ds(0, 49 - TAP_HALF), :]
    ggain[...] = tap_done[1, pl.ds(49 - TAP_HALF, 1), :]


def ring_shapes(n_lat, n_lon, rows, channels, low_first):
    own, got = [], []
    left = n_lat // 2
    while left > 1:
        pair = (left // 2, 2) if low_first else (2, left // 2)
        own.append(pltpu.VMEM(pair + (n_lon * rows, channels), F32))
        got.append(pltpu.VMEM((left // 2, n_lon * rows, channels), F32))
        left //= 2
    left = n_lon
    while left > 1:
        own.append(pltpu.VMEM((left // 2, 2, rows, channels), F32))
        got.append(pltpu.VMEM((left // 2, rows, channels), F32))
        left //= 2
    return own, got


def solution(mesh):
    n_lat, n_lon = mesh.shape["lat"], mesh.shape["lon"]

    def body(state, cot, taps, gain, w_in, w_out):
        height, width, channels = state.shape
        units = w_in.shape[1]
        cells = height * width
        rows = units // (n_lat * n_lon)
        block = n_lon * rows
        r_own, r_got = ring_shapes(n_lat, n_lon, rows, channels, True)
        l_own, l_got = ring_shapes(n_lat, n_lon, rows, channels, False)
        steps = len(r_own)
        wide = width + 2 * SIDE
        vmem = pl.BlockSpec(memory_space=pltpu.VMEM)
        dma = pltpu.SemaphoreType.DMA
        results = pl.pallas_call(
            functools.partial(kernel, n_lat, n_lon),
            out_shape=(
                jax.ShapeDtypeStruct((height, width, channels), BF16),
                jax.ShapeDtypeStruct((height, width, channels), BF16),
                jax.ShapeDtypeStruct((rows, 2 * channels), F32),
                jax.ShapeDtypeStruct((49, channels), F32),
                jax.ShapeDtypeStruct((1, channels), F32),
            ),
            in_specs=[vmem] * 6,
            out_specs=[vmem] * 5,
            scratch_shapes=[
                pltpu.VMEM((height + 6, wide, channels), F32),
                pltpu.VMEM((2, 3, wide, channels), F32),
                pltpu.VMEM((7, height + 6, width, channels), F32),
                pltpu.VMEM((height + 6, wide, channels), F32),
                pltpu.VMEM((2, 3, wide, channels), F32),
                pltpu.VMEM((7, height + 6, width, channels), F32),
                pltpu.VMEM((height, width, channels), F32),
                pltpu.VMEM((cells, channels), F32),
                pltpu.VMEM((cells, 1), F32),
                pltpu.VMEM((cells, channels), BF16),
                pltpu.VMEM((cells, channels), BF16),
                pltpu.VMEM((cells, channels), F32),
                pltpu.VMEM((cells, channels), F32),
                pltpu.VMEM((3, 49, channels), F32),
                pltpu.VMEM((n_lat // 2, 2, block, 2 * channels), F32),
                pltpu.VMEM((n_lat // 2, block, 2 * channels), F32),
                pltpu.VMEM((2, TAP_HALF, channels), F32),
                pltpu.VMEM((TAP_HALF, channels), F32),
                pltpu.VMEM((steps, TAP_HALF, channels), F32),
                pltpu.VMEM((2, TAP_HALF, channels), F32),
                r_own, r_got, l_own, l_got,
                pltpu.VMEM((steps, TAP_HALF, channels), F32),
                dma((2, 8)), dma((2, 8)), dma((units // CHUNK,)), dma((units // CHUNK,)),
                dma((2, steps)), dma((2, steps)), dma((steps + 2,)), dma((steps + 2,)),
            ],
            compiler_params=pltpu.CompilerParams(
                collective_id=0, has_side_effects=True, vmem_limit_bytes=48 * 1024 * 1024
            ),
            name="block",
        )(state, cot, taps, gain.reshape(1, channels), w_in, w_out)
        out, gin, wgrad, gtaps, ggain = results
        return out, gin, wgrad, gtaps, ggain.reshape(channels)

    placed = (P("lat", "lon", None), P("lat", "lon", None), P(), P(), P(), P())
    return jax.shard_map(
        body,
        mesh=mesh,
        in_specs=placed,
        out_specs=(P("lat", "lon", None), P("lat", "lon", None), P(("lat", "lon"), None), P(), P()),
        check_vma=False,
    )
```

```python
import functools
import math

import jax
import jax.numpy as jnp
from jax import lax
from jax.experimental import pallas as pl
from jax.experimental.pallas import tpu as pltpu
from jax.sharding import PartitionSpec as P

MESH = pl.DeviceIdType.MESH
F32 = jnp.float32
BF16 = jnp.bfloat16
SIDE = 8
TAP_HALF = 32


def dot(left, right, dims):
    return lax.dot_general(left, right, (dims, ((), ())), preferred_element_type=F32)


def kernel(
    n_lat, n_lon,
    state_h, cot_h, taps_h, gain_h, w_in_h, w_out_h,
    out, gin, wgrad, gtaps, ggain,
    state, cot, taps, gain, w_in, w_out,
    ext, rims, shifts, gext, grims, gshifts, conv, centred_s, istd_s, normed_s, cot_s,
    branch_s, gnorm_s, ghid_s, turned, local_w, core_w, pair_own, pair_got, group_own, group_got,
    tap_mine, tap_far, tap_chip, tap_group, tap_done,
    load_sem, halo_send, halo_recv, core_send, core_recv, pair_send, pair_recv,
    group_send, group_recv, tap_send, tap_recv, spread_send, spread_recv,
):
    loads = [
        pltpu.make_async_copy(source, target, load_sem.at[number])
        for number, (source, target) in enumerate(
            (
                (state_h, state), (cot_h, cot), (taps_h, taps),
                (gain_h, gain), (w_in_h, w_in), (w_out_h, w_out),
            )
        )
    ]
    for load in loads:
        load.start()
    height, width, channels = state.shape
    cells = height * width
    units = w_in.shape[1]
    rows = units // (n_lat * n_lon)
    block = n_lon * rows
    subs = n_lat // 8
    members = subs * n_lon
    chunk_rows = units // 4
    lat, lon = lax.axis_index("lat"), lax.axis_index("lon")
    first, last = lat == 0, lat == n_lat - 1
    core = lax.rem(lat, 2)

    def wrap(value):
        return lax.rem(value + 2 * n_lon, n_lon)

    up_lat = jnp.where(first, 0, lat - 1)
    down_lat = jnp.where(last, n_lat - 1, lat + 1)
    up_off = jnp.where(first, n_lon // 2, 0)
    down_off = jnp.where(last, n_lon // 2, 0)
    up_side = jnp.where(first, 0, 1)
    down_side = jnp.where(last, 1, 0)

    high_y = lax.div(lat, n_lat // 2)
    high_x = lax.rem(lax.div(lat, n_lat // 4), 2)
    base = lat - lax.rem(lat, n_lat // 4) + core
    member = lax.rem(lax.div(lat, 2), subs) * n_lon + lon
    core_peer = (lat + 1 - 2 * core, lon)

    def chip_peer(code):
        there = lat
        if code & 1:
            there = there + (n_lat // 4) * (1 - 2 * high_x)
        if code & 2:
            there = there + (n_lat // 2) * (1 - 2 * high_y)
        return there, lon

    def group_peer(step):
        index = lax.rem(member + step, members)
        return index, (base + 2 * lax.div(index, n_lon), lax.rem(index, n_lon))

    peers = []
    for side in (-1, 0, 1):
        peers.append((up_lat, wrap(lon + up_off + side)))
        peers.append((down_lat, wrap(lon + down_off + side)))
    peers.append((lat, wrap(lon - 1)))
    peers.append((lat, wrap(lon + 1)))
    peers.append(core_peer)
    for code in range(1, 4):
        peers.append(chip_peer(code))
    for step in range(1, members):
        peers.append(group_peer(step)[1])
    barrier = pltpu.get_barrier_semaphore()
    for peer in peers:
        pl.semaphore_signal(barrier, inc=1, device_id=peer, device_id_type=MESH)
    pl.semaphore_wait(barrier, len(peers))

    def remote(source, target, send, recv, peer):
        return pltpu.make_async_remote_copy(
            src_ref=source, dst_ref=target, send_sem=send, recv_sem=recv,
            device_id=peer, device_id_type=MESH,
        )

    spans = ((-1, 0, SIDE), (0, 0, width), (1, width - SIDE, SIDE))
    places = ((-1, SIDE + width), (0, SIDE), (1, 0))

    def halo_copies(stage, source, whole, rim):
        copies = []
        for number, ((side, start, count), (_, place)) in enumerate(zip(spans, places)):
            for end, (peer_lat, off, slot) in enumerate(
                ((up_lat, up_off, up_side), (down_lat, down_off, down_side))
            ):
                begin = 0 if end == 0 else height - 3
                copies.append(
                    remote(
                        source.at[pl.ds(begin, 3), pl.ds(start, count)],
                        rim.at[slot, :, pl.ds(place, count)],
                        halo_send.at[stage, 2 * number + end],
                        halo_recv.at[stage, 2 * number + slot],
                        (peer_lat, wrap(lon + off + side)),
                    )
                )
        copies.append(
            remote(
                source.at[:, pl.ds(0, SIDE)], whole.at[pl.ds(3, height), pl.ds(SIDE + width, SIDE)],
                halo_send.at[stage, 6], halo_recv.at[stage, 6], (lat, wrap(lon - 1)),
            )
        )
        copies.append(
            remote(
                source.at[:, pl.ds(width - SIDE, SIDE)], whole.at[pl.ds(3, height), pl.ds(0, SIDE)],
                halo_send.at[stage, 7], halo_recv.at[stage, 7], (lat, wrap(lon + 1)),
            )
        )
        return copies

    def finish_halo(stage, source, whole, rim, shifted):
        copies = halo_copies(stage, source, whole, rim)
        for copy in copies:
            copy.wait_send()
        for copy in copies[6:]:
            copy.wait_recv()
        for number, ((_, start, count), (_, place)) in enumerate(zip(spans, places)):
            for slot in range(2):
                remote(
                    source.at[pl.ds(0, 3), pl.ds(start, count)],
                    rim.at[slot, :, pl.ds(place, count)],
                    halo_send.at[stage, 2 * number + slot],
                    halo_recv.at[stage, 2 * number + slot],
                    (lat, wrap(lon + 1)),
                ).wait_recv()
        for row in range(3):
            whole[row] = jnp.where(first, rim[0, 2 - row], rim[0, row])
            whole[height + 3 + row] = jnp.where(last, rim[1, 2 - row], rim[1, row])

        def shift_row(row, carry):
            for col in range(7):
                shifted[col, row] = whole[row, pl.ds(SIDE - 3 + col, width), :]
            return carry

        lax.fori_loop(0, height + 6, shift_row, 0)

    for copy in halo_copies(0, state_h, ext, rims):
        copy.start()

    for load in loads:
        load.wait()
    ext[pl.ds(3, height), pl.ds(SIDE, width), :] = state[...]
    cot_s[...] = cot[...].astype(F32).reshape(cells, channels).astype(BF16)
    for chunk in range(4):
        ghid_s[chunk] = dot(
            cot_s[...], w_out[pl.ds(chunk * chunk_rows, chunk_rows), :], ((1,), (1,))
        )
    for row in range(7):
        for col in range(7):
            plain = taps[pl.ds(48 - 7 * row - col, 1), :]
            mirrored = taps[pl.ds(7 * row + 6 - col, 1), :]
            spot = pl.ds(7 * row + col, 1)
            turned[0, spot, :] = jnp.where(first, mirrored, plain)
            turned[1, spot, :] = plain
            turned[2, spot, :] = jnp.where(last, mirrored, plain)

    finish_halo(0, state_h, ext, rims, shifts)

    def conv_row(index, carry):
        total = jnp.zeros((width, channels), F32)
        for row in range(7):
            for col in range(7):
                total = total + shifts[col, index + row] * taps[pl.ds(7 * row + col, 1), :]
        conv[index] = total
        return carry

    lax.fori_loop(0, height, conv_row, 0)

    flat = conv[...].reshape(cells, channels)
    raw = flat - jnp.mean(flat, axis=-1, keepdims=True)
    inv_std = 1.0 / jnp.sqrt(jnp.mean(raw * raw, axis=-1, keepdims=True) + 1e-06)
    centred = raw * inv_std
    istd_s[...] = inv_std
    centred_s[...] = centred
    normed_s[...] = (centred * gain[...]).astype(BF16)

    def core_copy(turn):
        return remote(
            local_w.at[turn, :, 1 - core], core_w.at[turn],
            core_send.at[turn], core_recv.at[turn], core_peer,
        )

    def pair_copy(stream, slot):
        along_x = (stream == 0) == (slot < 2)
        return remote(
            pair_own.at[stream, slot], pair_got.at[stream, slot],
            pair_send.at[stream, slot], pair_recv.at[stream, slot],
            chip_peer(1) if along_x else chip_peer(2),
        )

    def core_sum(turn, stream):
        span = pl.ds(channels * (1 - stream), channels)
        return local_w[turn, :, core, :, span] + core_w[turn, :, :, span]

    def send_pair(stream, slot, value):
        pair_own[stream, slot] = value
        pair_copy(stream, slot).start()

    orders = ((1 - high_y, 1 - high_x), (high_y, 1 - high_x), (1 - high_y, high_x), (high_y, high_x))

    for turn, (part_y, part_x) in enumerate(orders):
        chunk = 2 * part_y + part_x
        span = pl.ds(pl.multiple_of(chunk * chunk_rows, chunk_rows), chunk_rows)
        into = w_in[:, span]
        outof = w_out[span, :]
        pre = dot(normed_s[...], into, ((1,), (0,)))
        share = 0.5 * (1.0 + lax.erf(pre * 0.7071067811865476))
        hidden = (pre * share).astype(BF16)
        slope = share + pre * jnp.exp(-0.5 * pre * pre) * 0.3989422804014327
        grad_pre = (ghid_s[chunk] * slope).astype(BF16)
        right = dot(hidden, cot_s[...], ((0,), (0,)))
        local_w[turn, :, :, :, pl.ds(channels, channels)] = right.reshape(subs, 2, block, channels)
        left = dot(grad_pre, normed_s[...], ((0,), (0,)))
        local_w[turn, :, :, :, pl.ds(0, channels)] = left.reshape(subs, 2, block, channels)
        core_copy(turn).start()
        branch = dot(hidden, outof, ((1,), (0,)))
        gnorm = dot(grad_pre, into, ((1,), (1,)))
        if turn == 0:
            branch_s[...] = branch
            gnorm_s[...] = gnorm
        else:
            branch_s[...] += branch
            gnorm_s[...] += gnorm
            core_copy(turn - 1).wait()
        if turn == 1:
            send_pair(0, 0, core_sum(0, 0))
            send_pair(1, 0, core_sum(0, 1))
        if turn == 2:
            send_pair(0, 1, core_sum(1, 0))
            pair_copy(1, 0).wait()
            send_pair(1, 2, core_sum(1, 1) + pair_got[1, 0])
        if turn == 3:
            send_pair(1, 1, core_sum(2, 1))
            pair_copy(0, 0).wait()
            send_pair(0, 2, core_sum(2, 0) + pair_got[0, 0])

    gnorm = gnorm_s[...]
    centred = centred_s[...]
    scaled = gnorm * gain[...]
    grad_conv = istd_s[...] * (
        scaled
        - jnp.mean(scaled, axis=-1, keepdims=True)
        - centred * jnp.mean(scaled * centred, axis=-1, keepdims=True)
    )
    conv[...] = grad_conv.reshape(height, width, channels)
    for copy in halo_copies(1, conv, gext, grims):
        copy.start()
    gext[pl.ds(3, height), pl.ds(SIDE, width), :] = conv[...]
    tap_mine[1, pl.ds(TAP_HALF // 2, TAP_HALF // 2), :] = jnp.zeros((TAP_HALF // 2, channels), F32)
    tap_mine[1, pl.ds(49 - TAP_HALF, 1), :] = jnp.sum(gnorm * centred, axis=0, keepdims=True)

    core_copy(3).wait()
    for stream in range(2):
        pair_copy(stream, 1).wait()
        pair_copy(stream, 2).wait()
        whole = core_sum(3, stream) + pair_got[stream, 1] + pair_got[stream, 2]
        for sub in range(subs):
            for part in range(n_lon):
                group_own[sub * n_lon + part, :, pl.ds(channels * (1 - stream), channels)] = whole[
                    sub, rows * part : rows * (part + 1)
                ]

    def group_copy(step):
        index, peer = group_peer(step)
        return remote(
            group_own.at[index], group_got.at[step - 1],
            group_send.at[step - 1], group_recv.at[step - 1], peer,
        )

    for step in range(1, members):
        group_copy(step).start()

    def tap_row(index, carry):
        row, col = lax.div(index, 7), lax.rem(index, 7)
        total = jnp.zeros((width, channels), F32)
        for line in range(height):
            total = total + shifts[col, row + line] * conv[line]
        tap_mine[lax.div(index, TAP_HALF), pl.ds(lax.rem(index, TAP_HALF), 1), :] = jnp.sum(
            total, axis=0, keepdims=True
        )
        return carry

    lax.fori_loop(0, 49, tap_row, 0)
    tap_first = remote(
        tap_mine.at[1 - core], tap_far, tap_send.at[0], tap_recv.at[0], core_peer
    )
    tap_first.start()

    out[...] = (
        state[...] + branch_s[...].reshape(height, width, channels)
    ).astype(BF16)
    finish_halo(1, conv, gext, grims, gshifts)

    tap_first.wait()
    quarter = 2 * high_y + high_x
    tap_chip[quarter] = tap_mine[core] + tap_far[...]

    def chip_copy(code):
        return remote(
            tap_chip.at[quarter], tap_chip.at[quarter],
            tap_send.at[1 + code], tap_recv.at[1 + code], chip_peer(code),
        )

    for code in range(1, 4):
        chip_copy(code).start()

    def adjoint_row(index, carry):
        total = jnp.zeros((width, channels), F32)
        for row in range(7):
            line = index + row
            kind = jnp.where(line < 3, 0, jnp.where(line >= height + 3, 2, 1))
            for col in range(7):
                total = total + gshifts[col, line] * turned[kind, pl.ds(7 * row + col, 1), :]
        ext[index, pl.ds(0, width), :] = total
        return carry

    lax.fori_loop(0, height // 2, adjoint_row, 0)

    for code in range(1, 4):
        chip_copy(code).wait()
    tap_group[member] = (tap_chip[0] + tap_chip[1]) + (tap_chip[2] + tap_chip[3])

    def spread_copy(step):
        _, peer = group_peer(step)
        return remote(
            tap_group.at[member], tap_group.at[member],
            spread_send.at[step - 1], spread_recv.at[step - 1], peer,
        )

    for step in range(1, members):
        spread_copy(step).start()

    lax.fori_loop(height // 2, height, adjoint_row, 0)

    scale = 1.0 / math.sqrt(cells * n_lat * n_lon)
    for step in range(1, members):
        group_copy(step).wait()
    total = group_own[member]
    for step in range(1, members):
        total = total + group_got[step - 1]
    wgrad[...] = total * scale

    for step in range(1, members):
        spread_copy(step).wait()
    total = tap_group[0]
    for step in range(1, members):
        total = total + tap_group[step]
    tap_done[core] = total * scale
    tap_last = remote(
        tap_done.at[core], tap_done.at[core], tap_send.at[1], tap_recv.at[1], core_peer
    )
    tap_last.start()
    gin[...] = (cot[...].astype(F32) + ext[pl.ds(0, height), pl.ds(0, width), :]).astype(BF16)
    tap_last.wait()
    gtaps[pl.ds(0, TAP_HALF), :] = tap_done[0]
    gtaps[pl.ds(TAP_HALF, 49 - TAP_HALF), :] = tap_done[1, pl.ds(0, 49 - TAP_HALF), :]
    ggain[...] = tap_done[1, pl.ds(49 - TAP_HALF, 1), :]


def solution(mesh):
    n_lat, n_lon = mesh.shape["lat"], mesh.shape["lon"]

    def body(state, cot, taps, gain, w_in, w_out):
        height, width, channels = state.shape
        units = w_in.shape[1]
        cells = height * width
        rows = units // (n_lat * n_lon)
        block = n_lon * rows
        subs = n_lat // 8
        members = subs * n_lon
        wide = width + 2 * SIDE
        vmem = pl.BlockSpec(memory_space=pltpu.VMEM)
        hbm = pl.BlockSpec(memory_space=pl.ANY)
        dma = pltpu.SemaphoreType.DMA
        args = (state, cot, taps, gain.reshape(1, channels), w_in, w_out)
        results = pl.pallas_call(
            functools.partial(kernel, n_lat, n_lon),
            out_shape=(
                jax.ShapeDtypeStruct((height, width, channels), BF16),
                jax.ShapeDtypeStruct((height, width, channels), BF16),
                jax.ShapeDtypeStruct((rows, 2 * channels), F32),
                jax.ShapeDtypeStruct((49, channels), F32),
                jax.ShapeDtypeStruct((1, channels), F32),
            ),
            in_specs=[hbm] * 6,
            out_specs=[vmem] * 5,
            scratch_shapes=[pltpu.VMEM(arg.shape, arg.dtype) for arg in args] + [
                pltpu.VMEM((height + 6, wide, channels), F32),
                pltpu.VMEM((2, 3, wide, channels), F32),
                pltpu.VMEM((7, height + 6, width, channels), F32),
                pltpu.VMEM((height + 6, wide, channels), F32),
                pltpu.VMEM((2, 3, wide, channels), F32),
                pltpu.VMEM((7, height + 6, width, channels), F32),
                pltpu.VMEM((height, width, channels), F32),
                pltpu.VMEM((cells, channels), F32),
                pltpu.VMEM((cells, 1), F32),
                pltpu.VMEM((cells, channels), BF16),
                pltpu.VMEM((cells, channels), BF16),
                pltpu.VMEM((cells, channels), F32),
                pltpu.VMEM((cells, channels), F32),
                pltpu.VMEM((4, cells, units // 4), F32),
                pltpu.VMEM((3, 49, channels), F32),
                pltpu.VMEM((4, subs, 2, block, 2 * channels), F32),
                pltpu.VMEM((4, subs, block, 2 * channels), F32),
                pltpu.VMEM((2, 3, subs, block, channels), F32),
                pltpu.VMEM((2, 3, subs, block, channels), F32),
                pltpu.VMEM((members, rows, 2 * channels), F32),
                pltpu.VMEM((members - 1, rows, 2 * channels), F32),
                pltpu.VMEM((2, TAP_HALF, channels), F32),
                pltpu.VMEM((TAP_HALF, channels), F32),
                pltpu.VMEM((4, TAP_HALF, channels), F32),
                pltpu.VMEM((members, TAP_HALF, channels), F32),
                pltpu.VMEM((2, TAP_HALF, channels), F32),
                dma((6,)), dma((2, 8)), dma((2, 8)), dma((4,)), dma((4,)), dma((2, 3)), dma((2, 3)),
                dma((members - 1,)), dma((members - 1,)), dma((5,)), dma((5,)),
                dma((members - 1,)), dma((members - 1,)),
            ],
            compiler_params=pltpu.CompilerParams(
                collective_id=0, has_side_effects=True, vmem_limit_bytes=60 * 1024 * 1024
            ),
            name="block",
        )(*args)
        out, gin, wgrad, gtaps, ggain = results
        return out, gin, wgrad, gtaps, ggain.reshape(channels)

    placed = (P("lat", "lon", None), P("lat", "lon", None), P(), P(), P(), P())
    return jax.shard_map(
        body,
        mesh=mesh,
        in_specs=placed,
        out_specs=(P("lat", "lon", None), P("lat", "lon", None), P(("lat", "lon"), None), P(), P()),
        check_vma=False,
    )
```

```python
import functools
import math

import jax
import jax.numpy as jnp
from jax import lax
from jax.experimental import pallas as pl
from jax.experimental.pallas import tpu as pltpu
from jax.sharding import PartitionSpec as P

MESH = pl.DeviceIdType.MESH
F32 = jnp.float32
BF16 = jnp.bfloat16
SIDE = 8


def dot(left, right, dims):
    return lax.dot_general(left, right, (dims, ((), ())), preferred_element_type=F32)


def kernel(
    n_lat, n_lon,
    state_h, cot_h, taps_h, gain_h, w_in_h, w_out_h,
    out, gin, wgrad, gtaps, ggain,
    state, cot, taps, gain, w_in, w_out,
    ext, rims, shifts, gext, grims, gshifts, conv, centred_s, istd_s, normed_s, cot_s,
    branch_s, gnorm_s, ghid_s, turned, local_w, core_w, pair_own, pair_got, group_own, group_got,
    side_own, side_got, tap_mine, tap_far, tap_done,
    load_sem, halo_send, halo_recv, core_send, core_recv, pair_send, pair_recv,
    group_send, group_recv, tap_send, tap_recv, spread_send, spread_recv,
):
    loads = [
        pltpu.make_async_copy(source, target, load_sem.at[number])
        for number, (source, target) in enumerate(
            (
                (state_h, state), (cot_h, cot), (taps_h, taps),
                (gain_h, gain), (w_in_h, w_in), (w_out_h, w_out),
            )
        )
    ]
    for load in loads:
        load.start()
    height, width, channels = state.shape
    cells = height * width
    pairs = height // 2
    units = w_in.shape[1]
    rows = units // (n_lat * n_lon)
    block = n_lon * rows
    share_rows = -(-50 // (n_lat * n_lon))
    subs = n_lat // 8
    members = subs * n_lon
    chunk_rows = units // 4
    lat, lon = lax.axis_index("lat"), lax.axis_index("lon")
    first, last = lat == 0, lat == n_lat - 1
    core = lax.rem(lat, 2)

    def wrap(value):
        return lax.rem(value + 2 * n_lon, n_lon)

    up_lat = jnp.where(first, 0, lat - 1)
    down_lat = jnp.where(last, n_lat - 1, lat + 1)
    up_off = jnp.where(first, n_lon // 2, 0)
    down_off = jnp.where(last, n_lon // 2, 0)
    up_side = jnp.where(first, 0, 1)
    down_side = jnp.where(last, 1, 0)

    high_y = lax.div(lat, n_lat // 2)
    high_x = lax.rem(lax.div(lat, n_lat // 4), 2)
    base = lat - lax.rem(lat, n_lat // 4) + core
    member = lax.rem(lax.div(lat, 2), subs) * n_lon + lon
    core_peer = (lat + 1 - 2 * core, lon)

    def chip_peer(code):
        there = lat
        if code & 1:
            there = there + (n_lat // 4) * (1 - 2 * high_x)
        if code & 2:
            there = there + (n_lat // 2) * (1 - 2 * high_y)
        return there, lon

    def group_peer(step):
        index = lax.rem(member + step, members)
        return index, (base + 2 * lax.div(index, n_lon), lax.rem(index, n_lon))

    devices = n_lat * n_lon
    flat_id = lat * n_lon + lon

    def device_at(step):
        index = lax.rem(flat_id + step, devices)
        return index, (lax.div(index, n_lon), lax.rem(index, n_lon))

    barrier = pltpu.get_barrier_semaphore()

    def greet(step, carry):
        pl.semaphore_signal(
            barrier, inc=1, device_id=device_at(step)[1], device_id_type=MESH
        )
        return carry

    lax.fori_loop(1, devices, greet, 0)
    loads[0].wait()
    pl.semaphore_wait(barrier, devices - 1)

    def remote(source, target, send, recv, peer):
        return pltpu.make_async_remote_copy(
            src_ref=source, dst_ref=target, send_sem=send, recv_sem=recv,
            device_id=peer, device_id_type=MESH,
        )

    spans = ((-1, 0, SIDE), (0, 0, width), (1, width - SIDE, SIDE))
    places = ((-1, SIDE + width), (0, SIDE), (1, 0))

    def halo_copies(stage, source, rim):
        copies = []
        for number, ((side, start, count), (_, place)) in enumerate(zip(spans, places)):
            for end, (peer_lat, off, slot) in enumerate(
                ((up_lat, up_off, up_side), (down_lat, down_off, down_side))
            ):
                begin = 0 if end == 0 else height - 3
                copies.append(
                    remote(
                        source.at[pl.ds(begin, 3), pl.ds(start, count)],
                        rim.at[slot, :, pl.ds(place, count)],
                        halo_send.at[stage, 2 * number + end],
                        halo_recv.at[stage, 2 * number + slot],
                        (peer_lat, wrap(lon + off + side)),
                    )
                )
        for toward in range(2):
            copies.append(
                remote(
                    side_own.at[stage, toward], side_got.at[stage, toward],
                    halo_send.at[stage, 6 + toward], halo_recv.at[stage, 6 + toward],
                    (lat, wrap(lon - 1 + 2 * toward)),
                )
            )
        return copies

    def start_halo(stage, source, local, rim):
        copies = halo_copies(stage, source, rim)
        for copy in copies[:6]:
            copy.start()
        for toward in range(2):
            span = pl.ds(toward * (width - 4), 4)
            for row in range(pairs):
                side_own[stage, toward, row, pl.ds(0, 4), :] = local[row, span, :]
                side_own[stage, toward, row, pl.ds(4, 4), :] = local[row + pairs, span, :]
            copies[6 + toward].start()

    def finish_halo(stage, source, whole, rim, shifted):
        copies = halo_copies(stage, source, rim)
        for copy in copies:
            copy.wait_send()
        for copy in copies[6:]:
            copy.wait_recv()
        for number, ((_, start, count), (_, place)) in enumerate(zip(spans, places)):
            for slot in range(2):
                remote(
                    source.at[pl.ds(0, 3), pl.ds(start, count)],
                    rim.at[slot, :, pl.ds(place, count)],
                    halo_send.at[stage, 2 * number + slot],
                    halo_recv.at[stage, 2 * number + slot],
                    (lat, wrap(lon + 1)),
                ).wait_recv()
        for toward, begin in ((0, SIDE + width), (1, SIDE - 4)):
            span = pl.ds(begin, 4)
            for row in range(pairs):
                whole[3 + row, span, :] = side_got[stage, toward, row, pl.ds(0, 4), :]
                whole[3 + row + pairs, span, :] = side_got[stage, toward, row, pl.ds(4, 4), :]
        for row in range(3):
            whole[row] = jnp.where(first, rim[0, 2 - row], rim[0, row])
            whole[height + 3 + row] = jnp.where(last, rim[1, 2 - row], rim[1, row])

        def shift_row(row, carry):
            for col in range(7):
                shifted[col, row] = whole[row, pl.ds(SIDE - 3 + col, width), :]
            return carry

        lax.fori_loop(0, height + 6, shift_row, 0)

    start_halo(0, state_h, state, rims)

    for load in loads[1:]:
        load.wait()
    ext[pl.ds(3, height), pl.ds(SIDE, width), :] = state[...]
    cot_s[...] = cot[...].astype(F32).reshape(cells, channels).astype(BF16)
    for chunk in range(4):
        ghid_s[chunk] = dot(
            cot_s[...], w_out[pl.ds(chunk * chunk_rows, chunk_rows), :], ((1,), (1,))
        )
    for row in range(7):
        for col in range(7):
            plain = taps[pl.ds(48 - 7 * row - col, 1), :]
            mirrored = taps[pl.ds(7 * row + 6 - col, 1), :]
            spot = pl.ds(7 * row + col, 1)
            turned[0, spot, :] = jnp.where(first, mirrored, plain)
            turned[1, spot, :] = plain
            turned[2, spot, :] = jnp.where(last, mirrored, plain)

    finish_halo(0, state_h, ext, rims, shifts)

    def conv_row(index, carry):
        total = jnp.zeros((width, channels), F32)
        for row in range(7):
            for col in range(7):
                total = total + shifts[col, index + row] * taps[pl.ds(7 * row + col, 1), :]
        conv[index] = total
        return carry

    lax.fori_loop(0, height, conv_row, 0)

    flat = conv[...].reshape(cells, channels)
    raw = flat - jnp.mean(flat, axis=-1, keepdims=True)
    inv_std = 1.0 / jnp.sqrt(jnp.mean(raw * raw, axis=-1, keepdims=True) + 1e-06)
    centred = raw * inv_std
    istd_s[...] = inv_std
    centred_s[...] = centred
    normed_s[...] = (centred * gain[...]).astype(BF16)

    def core_copy(turn):
        return remote(
            local_w.at[turn, :, 1 - core], core_w.at[turn],
            core_send.at[turn], core_recv.at[turn], core_peer,
        )

    def pair_copy(stream, slot):
        along_x = (stream == 0) == (slot < 2)
        return remote(
            pair_own.at[stream, slot], pair_got.at[stream, slot],
            pair_send.at[stream, slot], pair_recv.at[stream, slot],
            chip_peer(1) if along_x else chip_peer(2),
        )

    def core_sum(turn, stream):
        span = pl.ds(channels * (1 - stream), channels)
        return local_w[turn, :, core, :, span] + core_w[turn, :, :, span]

    def send_pair(stream, slot, value):
        pair_own[stream, slot] = value
        pair_copy(stream, slot).start()

    orders = ((1 - high_y, 1 - high_x), (high_y, 1 - high_x), (1 - high_y, high_x), (high_y, high_x))

    for turn, (part_y, part_x) in enumerate(orders):
        chunk = 2 * part_y + part_x
        span = pl.ds(pl.multiple_of(chunk * chunk_rows, chunk_rows), chunk_rows)
        into = w_in[:, span]
        outof = w_out[span, :]
        pre = dot(normed_s[...], into, ((1,), (0,)))
        share = 0.5 * (1.0 + lax.erf(pre * 0.7071067811865476))
        hidden = (pre * share).astype(BF16)
        slope = share + pre * jnp.exp(-0.5 * pre * pre) * 0.3989422804014327
        grad_pre = (ghid_s[chunk] * slope).astype(BF16)
        right = dot(hidden, cot_s[...], ((0,), (0,)))
        local_w[turn, :, :, :, pl.ds(channels, channels)] = right.reshape(subs, 2, block, channels)
        left = dot(grad_pre, normed_s[...], ((0,), (0,)))
        local_w[turn, :, :, :, pl.ds(0, channels)] = left.reshape(subs, 2, block, channels)
        core_copy(turn).start()
        branch = dot(hidden, outof, ((1,), (0,)))
        gnorm = dot(grad_pre, into, ((1,), (1,)))
        if turn == 0:
            branch_s[...] = branch
            gnorm_s[...] = gnorm
        else:
            branch_s[...] += branch
            gnorm_s[...] += gnorm
            core_copy(turn - 1).wait()
        if turn == 1:
            send_pair(0, 0, core_sum(0, 0))
            send_pair(1, 0, core_sum(0, 1))
        if turn == 2:
            send_pair(0, 1, core_sum(1, 0))
        if turn == 3:
            send_pair(1, 1, core_sum(2, 1))
            pair_copy(1, 0).wait()
            send_pair(1, 2, core_sum(1, 1) + pair_got[1, 0])

    gnorm = gnorm_s[...]
    centred = centred_s[...]
    scaled = gnorm * gain[...]
    grad_conv = istd_s[...] * (
        scaled
        - jnp.mean(scaled, axis=-1, keepdims=True)
        - centred * jnp.mean(scaled * centred, axis=-1, keepdims=True)
    )
    conv[...] = grad_conv.reshape(height, width, channels)
    start_halo(1, conv, conv, grims)
    pair_copy(0, 0).wait()
    send_pair(0, 2, core_sum(2, 0) + pair_got[0, 0])
    gext[pl.ds(3, height), pl.ds(SIDE, width), :] = conv[...]
    def store_tap(index, value):
        tap_mine[lax.div(index, share_rows), pl.ds(lax.rem(index, share_rows), 1), :] = value

    def tap_row(index, carry):
        row, col = lax.div(index, 7), lax.rem(index, 7)
        total = jnp.zeros((width, channels), F32)
        for line in range(height):
            total = total + shifts[col, row + line] * conv[line]
        store_tap(index, jnp.sum(total, axis=0, keepdims=True))
        return carry

    lax.fori_loop(0, 49, tap_row, 0)
    store_tap(49, jnp.sum(gnorm * centred, axis=0, keepdims=True))

    def clear_tap(index, carry):
        store_tap(index, jnp.zeros((1, channels), F32))
        return carry

    lax.fori_loop(50, share_rows * devices, clear_tap, 0)

    def scatter_copy(step):
        index, peer = device_at(step)
        return remote(
            tap_mine.at[index], tap_far.at[step - 1],
            tap_send.at[step - 1], tap_recv.at[step - 1], peer,
        )

    def gather_copy(step):
        _, peer = device_at(step)
        return remote(
            tap_done.at[flat_id], tap_done.at[flat_id],
            spread_send.at[step - 1], spread_recv.at[step - 1], peer,
        )

    def start_all(make):
        def begin(step, carry):
            make(step).start()
            return carry

        lax.fori_loop(1, devices, begin, 0)

    def wait_all(make):
        def finish(step, carry):
            make(step).wait()
            return carry

        lax.fori_loop(1, devices, finish, 0)

    start_all(scatter_copy)

    core_copy(3).wait()
    for stream in range(2):
        pair_copy(stream, 1).wait()
        pair_copy(stream, 2).wait()
        whole = core_sum(3, stream) + pair_got[stream, 1] + pair_got[stream, 2]
        for sub in range(subs):
            for part in range(n_lon):
                group_own[sub * n_lon + part, :, pl.ds(channels * (1 - stream), channels)] = whole[
                    sub, rows * part : rows * (part + 1)
                ]

    def group_copy(step):
        index, peer = group_peer(step)
        return remote(
            group_own.at[index], group_got.at[step - 1],
            group_send.at[step - 1], group_recv.at[step - 1], peer,
        )

    for step in range(1, members):
        group_copy(step).start()

    out[...] = (
        state[...] + branch_s[...].reshape(height, width, channels)
    ).astype(BF16)
    finish_halo(1, conv, gext, grims, gshifts)

    scale = 1.0 / math.sqrt(cells * devices)
    wait_all(scatter_copy)
    total = tap_mine[flat_id]
    total = total + jnp.sum(tap_far[...], axis=0)
    tap_done[flat_id] = total * scale
    start_all(gather_copy)

    def adjoint_row(index, carry):
        total = jnp.zeros((width, channels), F32)
        for row in range(7):
            line = index + row
            kind = jnp.where(line < 3, 0, jnp.where(line >= height + 3, 2, 1))
            for col in range(7):
                total = total + gshifts[col, line] * turned[kind, pl.ds(7 * row + col, 1), :]
        ext[index, pl.ds(0, width), :] = total
        return carry

    lax.fori_loop(0, height, adjoint_row, 0)
    gin[...] = (cot[...].astype(F32) + ext[pl.ds(0, height), pl.ds(0, width), :]).astype(BF16)

    for step in range(1, members):
        group_copy(step).wait()
    total = group_own[member]
    for step in range(1, members):
        total = total + group_got[step - 1]
    wgrad[...] = total * scale

    wait_all(gather_copy)
    for index in range(49):
        gtaps[pl.ds(index, 1), :] = tap_done[index // share_rows, pl.ds(index % share_rows, 1), :]
    ggain[...] = tap_done[49 // share_rows, pl.ds(49 % share_rows, 1), :]


def solution(mesh):
    n_lat, n_lon = mesh.shape["lat"], mesh.shape["lon"]

    def body(state, cot, taps, gain, w_in, w_out):
        height, width, channels = state.shape
        units = w_in.shape[1]
        cells = height * width
        rows = units // (n_lat * n_lon)
        block = n_lon * rows
        subs = n_lat // 8
        members = subs * n_lon
        devices = n_lat * n_lon
        share_rows = -(-50 // devices)
        wide = width + 2 * SIDE
        vmem = pl.BlockSpec(memory_space=pltpu.VMEM)
        hbm = pl.BlockSpec(memory_space=pl.ANY)
        dma = pltpu.SemaphoreType.DMA
        args = (state, cot, taps, gain.reshape(1, channels), w_in, w_out)
        results = pl.pallas_call(
            functools.partial(kernel, n_lat, n_lon),
            out_shape=(
                jax.ShapeDtypeStruct((height, width, channels), BF16),
                jax.ShapeDtypeStruct((height, width, channels), BF16),
                jax.ShapeDtypeStruct((rows, 2 * channels), F32),
                jax.ShapeDtypeStruct((49, channels), F32),
                jax.ShapeDtypeStruct((1, channels), F32),
            ),
            in_specs=[hbm] * 6,
            out_specs=[vmem] * 5,
            scratch_shapes=[pltpu.VMEM(arg.shape, arg.dtype) for arg in args] + [
                pltpu.VMEM((height + 6, wide, channels), F32),
                pltpu.VMEM((2, 3, wide, channels), F32),
                pltpu.VMEM((7, height + 6, width, channels), F32),
                pltpu.VMEM((height + 6, wide, channels), F32),
                pltpu.VMEM((2, 3, wide, channels), F32),
                pltpu.VMEM((7, height + 6, width, channels), F32),
                pltpu.VMEM((height, width, channels), F32),
                pltpu.VMEM((cells, channels), F32),
                pltpu.VMEM((cells, 1), F32),
                pltpu.VMEM((cells, channels), BF16),
                pltpu.VMEM((cells, channels), BF16),
                pltpu.VMEM((cells, channels), F32),
                pltpu.VMEM((cells, channels), F32),
                pltpu.VMEM((4, cells, units // 4), F32),
                pltpu.VMEM((3, 49, channels), F32),
                pltpu.VMEM((4, subs, 2, block, 2 * channels), F32),
                pltpu.VMEM((4, subs, block, 2 * channels), F32),
                pltpu.VMEM((2, 3, subs, block, channels), F32),
                pltpu.VMEM((2, 3, subs, block, channels), F32),
                pltpu.VMEM((members, rows, 2 * channels), F32),
                pltpu.VMEM((members - 1, rows, 2 * channels), F32),
                pltpu.VMEM((2, 2, height // 2, 8, channels), F32),
                pltpu.VMEM((2, 2, height // 2, 8, channels), F32),
                pltpu.VMEM((devices, share_rows, channels), F32),
                pltpu.VMEM((devices - 1, share_rows, channels), F32),
                pltpu.VMEM((devices, share_rows, channels), F32),
                dma((6,)), dma((2, 8)), dma((2, 8)), dma((4,)), dma((4,)), dma((2, 3)), dma((2, 3)),
                dma((members - 1,)), dma((members - 1,)), dma((devices - 1,)), dma((devices - 1,)),
                dma((devices - 1,)), dma((devices - 1,)),
            ],
            compiler_params=pltpu.CompilerParams(
                collective_id=0, has_side_effects=True, vmem_limit_bytes=60 * 1024 * 1024
            ),
            name="block",
        )(*args)
        out, gin, wgrad, gtaps, ggain = results
        return out, gin, wgrad, gtaps, ggain.reshape(channels)

    placed = (P("lat", "lon", None), P("lat", "lon", None), P(), P(), P(), P())
    return jax.shard_map(
        body,
        mesh=mesh,
        in_specs=placed,
        out_specs=(P("lat", "lon", None), P("lat", "lon", None), P(("lat", "lon"), None), P(), P()),
        check_vma=False,
    )
```

```python
import functools
import math

import jax
import jax.numpy as jnp
from jax import lax
from jax.experimental import pallas as pl
from jax.experimental.pallas import tpu as pltpu
from jax.sharding import PartitionSpec as P

MESH = pl.DeviceIdType.MESH
F32 = jnp.float32
BF16 = jnp.bfloat16
SIDE = 8
GROUP = 4


def dot(left, right, dims):
    return lax.dot_general(left, right, (dims, ((), ())), preferred_element_type=F32)


def kernel(
    n_lat, n_lon,
    state_h, cot_h, taps_h, gain_h, w_in_h, w_out_h,
    out, gin, wgrad, gtaps, ggain,
    state, cot, taps, gain, w_in, w_out,
    ext, rims, shifts, gext, grims, gshifts, conv, centred_s, istd_s, normed_s, cot_s,
    branch_s, gnorm_s, ghid_s, spread, turned, local_w, core_w, pair_own, pair_got, group_own, group_got,
    side_own, side_got, tap_mine, tap_far, tap_done,
    load_sem, halo_send, halo_recv, core_send, core_recv, pair_send, pair_recv,
    group_send, group_recv, tap_send, tap_recv, spread_send, spread_recv,
):
    loads = [
        pltpu.make_async_copy(source, target, load_sem.at[number])
        for number, (source, target) in enumerate(
            (
                (state_h, state), (cot_h, cot), (taps_h, taps),
                (gain_h, gain), (w_in_h, w_in), (w_out_h, w_out),
            )
        )
    ]
    for load in loads:
        load.start()
    height, width, channels = state.shape
    cells = height * width
    pairs = height // 2
    units = w_in.shape[1]
    rows = units // (n_lat * n_lon)
    block = n_lon * rows
    share_rows = -(-50 // (n_lat * n_lon))
    subs = n_lat // 8
    members = subs * n_lon
    chunk_rows = units // 4
    lat, lon = lax.axis_index("lat"), lax.axis_index("lon")
    first, last = lat == 0, lat == n_lat - 1
    core = lax.rem(lat, 2)

    def wrap(value):
        return lax.rem(value + 2 * n_lon, n_lon)

    up_lat = jnp.where(first, 0, lat - 1)
    down_lat = jnp.where(last, n_lat - 1, lat + 1)
    up_off = jnp.where(first, n_lon // 2, 0)
    down_off = jnp.where(last, n_lon // 2, 0)
    up_side = jnp.where(first, 0, 1)
    down_side = jnp.where(last, 1, 0)

    high_y = lax.div(lat, n_lat // 2)
    high_x = lax.rem(lax.div(lat, n_lat // 4), 2)
    base = lat - lax.rem(lat, n_lat // 4) + core
    member = lax.rem(lax.div(lat, 2), subs) * n_lon + lon
    core_peer = (lat + 1 - 2 * core, lon)

    def chip_peer(code):
        there = lat
        if code & 1:
            there = there + (n_lat // 4) * (1 - 2 * high_x)
        if code & 2:
            there = there + (n_lat // 2) * (1 - 2 * high_y)
        return there, lon

    def group_peer(step):
        index = lax.rem(member + step, members)
        return index, (base + 2 * lax.div(index, n_lon), lax.rem(index, n_lon))

    devices = n_lat * n_lon
    flat_id = lat * n_lon + lon

    def device_at(step):
        index = lax.rem(flat_id + step, devices)
        return index, (lax.div(index, n_lon), lax.rem(index, n_lon))

    barrier = pltpu.get_barrier_semaphore()

    def greet(step, carry):
        pl.semaphore_signal(
            barrier, inc=1, device_id=device_at(step)[1], device_id_type=MESH
        )
        return carry

    lax.fori_loop(1, devices, greet, 0)
    loads[0].wait()
    pl.semaphore_wait(barrier, devices - 1)

    def remote(source, target, send, recv, peer):
        return pltpu.make_async_remote_copy(
            src_ref=source, dst_ref=target, send_sem=send, recv_sem=recv,
            device_id=peer, device_id_type=MESH,
        )

    spans = ((-1, 0, SIDE), (0, 0, width), (1, width - SIDE, SIDE))
    places = ((-1, SIDE + width), (0, SIDE), (1, 0))

    def halo_copies(stage, source, rim):
        copies = []
        for number, ((side, start, count), (_, place)) in enumerate(zip(spans, places)):
            for end, (peer_lat, off, slot) in enumerate(
                ((up_lat, up_off, up_side), (down_lat, down_off, down_side))
            ):
                begin = 0 if end == 0 else height - 3
                copies.append(
                    remote(
                        source.at[pl.ds(begin, 3), pl.ds(start, count)],
                        rim.at[slot, :, pl.ds(place, count)],
                        halo_send.at[stage, 2 * number + end],
                        halo_recv.at[stage, 2 * number + slot],
                        (peer_lat, wrap(lon + off + side)),
                    )
                )
        for toward in range(2):
            copies.append(
                remote(
                    side_own.at[stage, toward], side_got.at[stage, toward],
                    halo_send.at[stage, 6 + toward], halo_recv.at[stage, 6 + toward],
                    (lat, wrap(lon - 1 + 2 * toward)),
                )
            )
        return copies

    def start_halo(stage, source, local, rim):
        copies = halo_copies(stage, source, rim)
        for copy in copies[:6]:
            copy.start()
        for toward in range(2):
            span = pl.ds(toward * (width - 4), 4)
            for row in range(pairs):
                side_own[stage, toward, row, pl.ds(0, 4), :] = local[row, span, :]
                side_own[stage, toward, row, pl.ds(4, 4), :] = local[row + pairs, span, :]
            copies[6 + toward].start()

    def finish_halo(stage, source, whole, rim, shifted):
        copies = halo_copies(stage, source, rim)
        for copy in copies:
            copy.wait_send()
        for copy in copies[6:]:
            copy.wait_recv()
        for number, ((_, start, count), (_, place)) in enumerate(zip(spans, places)):
            for slot in range(2):
                remote(
                    source.at[pl.ds(0, 3), pl.ds(start, count)],
                    rim.at[slot, :, pl.ds(place, count)],
                    halo_send.at[stage, 2 * number + slot],
                    halo_recv.at[stage, 2 * number + slot],
                    (lat, wrap(lon + 1)),
                ).wait_recv()
        for toward, begin in ((0, SIDE + width), (1, SIDE - 4)):
            span = pl.ds(begin, 4)
            for row in range(pairs):
                whole[3 + row, span, :] = side_got[stage, toward, row, pl.ds(0, 4), :]
                whole[3 + row + pairs, span, :] = side_got[stage, toward, row, pl.ds(4, 4), :]
        for row in range(3):
            whole[row] = jnp.where(first, rim[0, 2 - row], rim[0, row])
            whole[height + 3 + row] = jnp.where(last, rim[1, 2 - row], rim[1, row])

        def shift_row(row, carry):
            for col in range(7):
                shifted[col, row] = whole[row, pl.ds(SIDE - 3 + col, width), :]
            return carry

        lax.fori_loop(0, height + 6, shift_row, 0)

    start_halo(0, state_h, state, rims)

    for load in loads[1:]:
        load.wait()
    ext[pl.ds(3, height), pl.ds(SIDE, width), :] = state[...]
    cot_s[...] = cot[...].astype(F32).reshape(cells, channels).astype(BF16)
    for chunk in range(4):
        ghid_s[chunk] = dot(
            cot_s[...], w_out[pl.ds(chunk * chunk_rows, chunk_rows), :], ((1,), (1,))
        )
    for row in range(7):
        for col in range(7):
            wide_shape = (8, channels)
            forward = jnp.broadcast_to(taps[pl.ds(7 * row + col, 1), :], wide_shape)
            plain = jnp.broadcast_to(taps[pl.ds(48 - 7 * row - col, 1), :], wide_shape)
            mirrored = jnp.broadcast_to(taps[pl.ds(7 * row + 6 - col, 1), :], wide_shape)
            spot = 7 * row + col
            spread[spot] = forward
            turned[0, spot] = jnp.where(first, mirrored, plain)
            turned[1, spot] = plain
            turned[2, spot] = jnp.where(last, mirrored, plain)

    finish_halo(0, state_h, ext, rims, shifts)

    def filtered(source, weight_of, store):
        def step(group, carry):
            begin = group * GROUP
            totals = [jnp.zeros((width // 8, 8, channels), F32) for _ in range(GROUP)]
            for line in range(GROUP + 6):
                for col in range(7):
                    cells_in = source[col, begin + line].reshape(width // 8, 8, channels)
                    for out_row in range(GROUP):
                        if 0 <= line - out_row < 7:
                            totals[out_row] = totals[out_row] + cells_in * weight_of(
                                begin + line, line - out_row, col
                            )
            for out_row in range(GROUP):
                store(begin + out_row, totals[out_row].reshape(width, channels))
            return carry

        lax.fori_loop(0, height // GROUP, step, 0)

    def store_conv(row, value):
        conv[row] = value

    filtered(shifts, lambda line, row, col: spread[7 * row + col], store_conv)

    flat = conv[...].reshape(cells, channels)
    raw = flat - jnp.mean(flat, axis=-1, keepdims=True)
    inv_std = 1.0 / jnp.sqrt(jnp.mean(raw * raw, axis=-1, keepdims=True) + 1e-06)
    centred = raw * inv_std
    istd_s[...] = inv_std
    centred_s[...] = centred
    normed_s[...] = (centred * gain[...]).astype(BF16)

    def core_copy(turn):
        return remote(
            local_w.at[turn, :, 1 - core], core_w.at[turn],
            core_send.at[turn], core_recv.at[turn], core_peer,
        )

    def pair_copy(stream, slot):
        along_x = (stream == 0) == (slot < 2)
        return remote(
            pair_own.at[stream, slot], pair_got.at[stream, slot],
            pair_send.at[stream, slot], pair_recv.at[stream, slot],
            chip_peer(1) if along_x else chip_peer(2),
        )

    def core_sum(turn, stream):
        span = pl.ds(channels * (1 - stream), channels)
        return local_w[turn, :, core, :, span] + core_w[turn, :, :, span]

    def send_pair(stream, slot, value):
        pair_own[stream, slot] = value
        pair_copy(stream, slot).start()

    orders = ((1 - high_y, 1 - high_x), (high_y, 1 - high_x), (1 - high_y, high_x), (high_y, high_x))

    for turn, (part_y, part_x) in enumerate(orders):
        chunk = 2 * part_y + part_x
        span = pl.ds(pl.multiple_of(chunk * chunk_rows, chunk_rows), chunk_rows)
        into = w_in[:, span]
        outof = w_out[span, :]
        pre = dot(normed_s[...], into, ((1,), (0,)))
        share = 0.5 * (1.0 + lax.erf(pre * 0.7071067811865476))
        hidden = (pre * share).astype(BF16)
        slope = share + pre * jnp.exp(-0.5 * pre * pre) * 0.3989422804014327
        grad_pre = (ghid_s[chunk] * slope).astype(BF16)
        right = dot(hidden, cot_s[...], ((0,), (0,)))
        local_w[turn, :, :, :, pl.ds(channels, channels)] = right.reshape(subs, 2, block, channels)
        left = dot(grad_pre, normed_s[...], ((0,), (0,)))
        local_w[turn, :, :, :, pl.ds(0, channels)] = left.reshape(subs, 2, block, channels)
        core_copy(turn).start()
        branch = dot(hidden, outof, ((1,), (0,)))
        gnorm = dot(grad_pre, into, ((1,), (1,)))
        if turn == 0:
            branch_s[...] = branch
            gnorm_s[...] = gnorm
        else:
            branch_s[...] += branch
            gnorm_s[...] += gnorm
            core_copy(turn - 1).wait()
        if turn == 1:
            send_pair(0, 0, core_sum(0, 0))
            send_pair(1, 0, core_sum(0, 1))
        if turn == 2:
            send_pair(0, 1, core_sum(1, 0))
        if turn == 3:
            send_pair(1, 1, core_sum(2, 1))
            pair_copy(1, 0).wait()
            send_pair(1, 2, core_sum(1, 1) + pair_got[1, 0])

    gnorm = gnorm_s[...]
    centred = centred_s[...]
    scaled = gnorm * gain[...]
    grad_conv = istd_s[...] * (
        scaled
        - jnp.mean(scaled, axis=-1, keepdims=True)
        - centred * jnp.mean(scaled * centred, axis=-1, keepdims=True)
    )
    conv[...] = grad_conv.reshape(height, width, channels)
    start_halo(1, conv, conv, grims)
    pair_copy(0, 0).wait()
    send_pair(0, 2, core_sum(2, 0) + pair_got[0, 0])
    gext[pl.ds(3, height), pl.ds(SIDE, width), :] = conv[...]
    def store_tap(index, value):
        tap_mine[lax.div(index, share_rows), pl.ds(lax.rem(index, share_rows), 1), :] = value

    def tap_column(col, carry):
        totals = [jnp.zeros((8, channels), F32) for _ in range(7)]
        for line in range(height):
            grads = conv[line].reshape(width // 8, 8, channels)
            for row in range(7):
                terms = shifts[col, row + line].reshape(width // 8, 8, channels) * grads
                for part in range(width // 8):
                    totals[row] = totals[row] + terms[part]
        for row in range(7):
            store_tap(7 * row + col, jnp.sum(totals[row], axis=0, keepdims=True))
        return carry

    lax.fori_loop(0, 7, tap_column, 0)
    store_tap(49, jnp.sum(gnorm * centred, axis=0, keepdims=True))

    def clear_tap(index, carry):
        store_tap(index, jnp.zeros((1, channels), F32))
        return carry

    lax.fori_loop(50, share_rows * devices, clear_tap, 0)

    def scatter_copy(step):
        index, peer = device_at(step)
        return remote(
            tap_mine.at[index], tap_far.at[step - 1],
            tap_send.at[step - 1], tap_recv.at[step - 1], peer,
        )

    def gather_copy(step):
        _, peer = device_at(step)
        return remote(
            tap_done.at[flat_id], tap_done.at[flat_id],
            spread_send.at[step - 1], spread_recv.at[step - 1], peer,
        )

    def start_all(make):
        def begin(step, carry):
            make(step).start()
            return carry

        lax.fori_loop(1, devices, begin, 0)

    def wait_all(make):
        def finish(step, carry):
            make(step).wait()
            return carry

        lax.fori_loop(1, devices, finish, 0)

    start_all(scatter_copy)

    core_copy(3).wait()
    for stream in range(2):
        pair_copy(stream, 1).wait()
        pair_copy(stream, 2).wait()
        whole = core_sum(3, stream) + pair_got[stream, 1] + pair_got[stream, 2]
        for sub in range(subs):
            for part in range(n_lon):
                group_own[sub * n_lon + part, :, pl.ds(channels * (1 - stream), channels)] = whole[
                    sub, rows * part : rows * (part + 1)
                ]

    def group_copy(step):
        index, peer = group_peer(step)
        return remote(
            group_own.at[index], group_got.at[step - 1],
            group_send.at[step - 1], group_recv.at[step - 1], peer,
        )

    for step in range(1, members):
        group_copy(step).start()

    out[...] = (
        state[...] + branch_s[...].reshape(height, width, channels)
    ).astype(BF16)
    finish_halo(1, conv, gext, grims, gshifts)

    scale = 1.0 / math.sqrt(cells * devices)
    wait_all(scatter_copy)
    total = tap_mine[flat_id]
    total = total + jnp.sum(tap_far[...], axis=0)
    tap_done[flat_id] = total * scale
    start_all(gather_copy)

    def turned_at(line, row, col):
        kind = jnp.where(line < 3, 0, jnp.where(line >= height + 3, 2, 1))
        return turned[kind, 7 * row + col]

    def store_adjoint(row, value):
        ext[row, pl.ds(0, width), :] = value

    filtered(gshifts, turned_at, store_adjoint)
    gin[...] = (cot[...].astype(F32) + ext[pl.ds(0, height), pl.ds(0, width), :]).astype(BF16)

    for step in range(1, members):
        group_copy(step).wait()
    total = group_own[member]
    for step in range(1, members):
        total = total + group_got[step - 1]
    wgrad[...] = total * scale

    wait_all(gather_copy)
    for index in range(49):
        gtaps[pl.ds(index, 1), :] = tap_done[index // share_rows, pl.ds(index % share_rows, 1), :]
    ggain[...] = tap_done[49 // share_rows, pl.ds(49 % share_rows, 1), :]


def solution(mesh):
    n_lat, n_lon = mesh.shape["lat"], mesh.shape["lon"]

    def body(state, cot, taps, gain, w_in, w_out):
        height, width, channels = state.shape
        units = w_in.shape[1]
        cells = height * width
        rows = units // (n_lat * n_lon)
        block = n_lon * rows
        subs = n_lat // 8
        members = subs * n_lon
        devices = n_lat * n_lon
        share_rows = -(-50 // devices)
        wide = width + 2 * SIDE
        vmem = pl.BlockSpec(memory_space=pltpu.VMEM)
        hbm = pl.BlockSpec(memory_space=pltpu.HBM)
        dma = pltpu.SemaphoreType.DMA
        args = (state, cot, taps, gain.reshape(1, channels), w_in, w_out)
        results = pl.pallas_call(
            functools.partial(kernel, n_lat, n_lon),
            out_shape=(
                jax.ShapeDtypeStruct((height, width, channels), BF16),
                jax.ShapeDtypeStruct((height, width, channels), BF16),
                jax.ShapeDtypeStruct((rows, 2 * channels), F32),
                jax.ShapeDtypeStruct((49, channels), F32),
                jax.ShapeDtypeStruct((1, channels), F32),
            ),
            in_specs=[hbm] * 6,
            out_specs=[vmem] * 5,
            scratch_shapes=[pltpu.VMEM(arg.shape, arg.dtype) for arg in args] + [
                pltpu.VMEM((height + 6, wide, channels), F32),
                pltpu.VMEM((2, 3, wide, channels), F32),
                pltpu.VMEM((7, height + 6, width, channels), F32),
                pltpu.VMEM((height + 6, wide, channels), F32),
                pltpu.VMEM((2, 3, wide, channels), F32),
                pltpu.VMEM((7, height + 6, width, channels), F32),
                pltpu.VMEM((height, width, channels), F32),
                pltpu.VMEM((cells, channels), F32),
                pltpu.VMEM((cells, 1), F32),
                pltpu.VMEM((cells, channels), BF16),
                pltpu.VMEM((cells, channels), BF16),
                pltpu.VMEM((cells, channels), F32),
                pltpu.VMEM((cells, channels), F32),
                pltpu.VMEM((4, cells, units // 4), F32),
                pltpu.VMEM((49, 8, channels), F32),
                pltpu.VMEM((3, 49, 8, channels), F32),
                pltpu.VMEM((4, subs, 2, block, 2 * channels), F32),
                pltpu.VMEM((4, subs, block, 2 * channels), F32),
                pltpu.VMEM((2, 3, subs, block, channels), F32),
                pltpu.VMEM((2, 3, subs, block, channels), F32),
                pltpu.VMEM((members, rows, 2 * channels), F32),
                pltpu.VMEM((members - 1, rows, 2 * channels), F32),
                pltpu.VMEM((2, 2, height // 2, 8, channels), F32),
                pltpu.VMEM((2, 2, height // 2, 8, channels), F32),
                pltpu.VMEM((devices, share_rows, channels), F32),
                pltpu.VMEM((devices - 1, share_rows, channels), F32),
                pltpu.VMEM((devices, share_rows, channels), F32),
                dma((6,)), dma((2, 8)), dma((2, 8)), dma((4,)), dma((4,)), dma((2, 3)), dma((2, 3)),
                dma((members - 1,)), dma((members - 1,)), dma((devices - 1,)), dma((devices - 1,)),
                dma((devices - 1,)), dma((devices - 1,)),
            ],
            compiler_params=pltpu.CompilerParams(
                collective_id=0, has_side_effects=True, vmem_limit_bytes=40 * 1024 * 1024
            ),
            name="block",
        )(*args)
        out, gin, wgrad, gtaps, ggain = results
        return out, gin, wgrad, gtaps, ggain.reshape(channels)

    placed = (P("lat", "lon", None), P("lat", "lon", None), P(), P(), P(), P())
    return jax.shard_map(
        body,
        mesh=mesh,
        in_specs=placed,
        out_specs=(P("lat", "lon", None), P("lat", "lon", None), P(("lat", "lon"), None), P(), P()),
        check_vma=False,
    )
```
